32 devices in a mesh: dom: 8 (over z, core), band: 4 (over y, x).
Axes of the slice: x: 2, y: 2, z: 4, core: 2. Of those that a mesh axis runs over, the one named last changes fastest.
Arguments:
- block: float32 [16384, 256], P('dom', 'band'), may hold values from -8 to 8
- locked: float32 [16384, 8192], P('dom', 'band'), may hold values from -1.1 to 1.1
Outputs:
- basis: float32 [16384, 256], P('dom', 'band')
- coefficients: float32 [8192, 256], P('band')
The draws below stay inside these ranges and needn't reach their ends.
All inputs are finite; a program needn't handle non-finite values.
Results may differ from the reference program's by a relative error of at most 0.0003.
Values sent between devices are 32-bit elements; how exact they have to be, the bound alone decides.
No kernel may reach another device: no remote copies, remote signals or barrier semaphores. Data moves between devices by JAX's collectives and lax.ppermute only.
A program may use at most 64 MiB of HBM per device.

```python
import math
import jax
import jax.numpy as jnp
from jax import lax

NQ = 8192
NB = 256
ROWS = 16384


def cosine_table(count):
    place = jnp.arange(count, dtype=jnp.int32)
    freq = jnp.arange(count, dtype=jnp.int32)
    phase = (2 * place[:, None] + 1) * freq[None, :] % (4 * count)
    table = jnp.cos(jnp.float32(math.pi) * phase.astype(jnp.float32) / jnp.float32(2 * count))
    scales = jnp.where(freq == 0, jnp.float32(math.sqrt(1.0 / count)), jnp.float32(math.sqrt(2.0 / count)))
    return (table * scales[None, :]).astype(jnp.float32)


def random_signs(key, count):
    return (2 * jax.random.randint(key, (count,), 0, 2) - 1).astype(jnp.float32)


def unit_columns(key):
    side = math.gcd(ROWS, 128)
    outer = ROWS // side
    keys = jax.random.split(key, 4)
    picked = jax.random.permutation(keys[0], ROWS)[:NQ]
    outer_table = cosine_table(outer)
    side_table = cosine_table(side)
    start = outer_table[:, picked // side][:, None, :] * side_table[:, picked % side][None, :, :]
    start = start.reshape(ROWS, NQ) * random_signs(keys[1], NQ)[None, :]
    order = jax.random.permutation(keys[2], ROWS)
    mixed = (start * random_signs(keys[3], ROWS)[:, None])[order]
    mixed = mixed.reshape(outer, side, NQ)
    mixed = jnp.einsum('ia,abn->ibn', outer_table, mixed, precision=lax.Precision.HIGHEST)
    mixed = jnp.einsum('jb,ibn->ijn', side_table, mixed, precision=lax.Precision.HIGHEST)
    return mixed.reshape(ROWS, NQ)


def locked_columns(key):
    base = jax.random.fold_in(key, 7101)
    keys = jax.random.split(base, 4)
    unit = unit_columns(keys[0])
    cycle = jax.random.permutation(keys[1], NQ)
    back = jnp.argsort(cycle, stable=True)
    tilt = jnp.exp(jax.random.uniform(keys[2], (NQ,), minval=math.log(0.02), maxval=math.log(0.2)))
    tilt = tilt * random_signs(keys[3], NQ)
    ordered = unit[:, cycle]
    partner = jnp.roll(ordered, -1, axis=1)
    tilted = ordered + tilt[cycle][None, :] * partner
    return tilted[:, back].astype(jnp.float32)


def draw_locked(key, part):
    return locked_columns(key)


def draw_block(key, part):
    locked = locked_columns(key)
    keys = jax.random.split(jax.random.fold_in(key, 7202), 4)
    col_scale = jnp.exp(jax.random.uniform(keys[2], (NB,), minval=math.log(0.05), maxval=math.log(0.5)))
    mixing = jnp.clip(jax.random.normal(keys[0], (NQ, NB)), -4.0, 4.0)
    noise = jnp.clip(jax.random.normal(keys[1], (ROWS, NB)), -4.0, 4.0)
    common = jnp.clip(jax.random.normal(keys[3], (ROWS,)), -4.0, 4.0)
    rest = (noise + 0.7 * common[:, None]) * col_scale[None, :]
    block = jnp.dot(locked, mixing, precision=lax.Precision.HIGHEST) + rest
    return jnp.clip(block, -8.0, 8.0).astype(jnp.float32)


def setup_inputs(seed: int = 0) -> dict:
    key_list = jax.random.split(jax.random.key(seed), 3)
    block = draw_block(jax.random.fold_in(key_list[2], 71), 0)
    locked = draw_locked(jax.random.fold_in(key_list[2], 71), 0)
    return {"block": block, "locked": locked}


def project(locked, current):
    coef = lax.dot_general(locked.astype(jnp.float32), current.astype(jnp.float32), (((0,), (0,)), ((), ())), precision=lax.Precision.HIGHEST, preferred_element_type=jnp.float32)
    after = current - jnp.dot(locked.astype(jnp.float32), coef.astype(jnp.float32), precision=lax.Precision.HIGHEST, preferred_element_type=jnp.float32)
    return (coef, after)

def reference(block, locked):
    first, once = project(locked, block)
    second, twice = project(locked, once)
    coefficients = first + second
    gram = jnp.dot(twice.T.astype(jnp.float32), twice.astype(jnp.float32), precision=lax.Precision.HIGHEST, preferred_element_type=jnp.float32) / ROWS
    lower = jnp.linalg.cholesky(gram)
    basis = jax.scipy.linalg.solve_triangular(lower, twice.T, lower=True).T
    return (basis, coefficients)
```

```python
import jax
import jax.numpy as jnp
from jax import lax
from jax.sharding import PartitionSpec as P

CHUNKS = 2
f32 = jnp.float32


def swap(x, axis, k):
    n = lax.axis_size(axis)
    return lax.ppermute(x, axis, [(i, i ^ k) for i in range(n)])


def bits(n):
    return [1 << i for i in range(n.bit_length() - 1)]


def split(x):
    hi = lax.reduce_precision(x, 8, 7)
    return hi.astype(jnp.bfloat16), (x - hi).astype(jnp.bfloat16)


def product(parts, w, dim):
    high, low = parts
    w_high, w_low = split(w)
    n = w.shape[0]
    dims = (((1,), (dim,)), ((), ()))
    both = lax.dot_general(
        jnp.concatenate([w_high, w_low], 0), high, dims, preferred_element_type=f32
    )
    rest = lax.dot_general(w_high, low, dims, preferred_element_type=f32)
    return both[:n] + (both[n:] + rest)


def halve(x, axis, k, dim):
    half = x.shape[dim] // 2
    bit = (lax.axis_index(axis) // k) % 2
    send = lax.dynamic_slice_in_dim(x, (1 - bit) * half, half, dim)
    keep = lax.dynamic_slice_in_dim(x, bit * half, half, dim)
    return keep + swap(send, axis, k)


def double(x, axis, k, dim):
    bit = (lax.axis_index(axis) // k) % 2 == 1
    other = swap(x, axis, k)
    return jnp.concatenate([jnp.where(bit, other, x), jnp.where(bit, x, other)], dim)


def dom_sum(x):
    ks = bits(lax.axis_size("dom"))
    for k in ks:
        x = halve(x, "dom", k, 0)
    for k in reversed(ks):
        x = double(x, "dom", k, 0)
    return x


def scatter_direct(x, axis, dim):
    n = lax.axis_size(axis)
    me = lax.axis_index(axis)
    piece = x.shape[dim] // n
    total = lax.dynamic_slice_in_dim(x, me * piece, piece, dim)
    got = [
        swap(lax.dynamic_slice_in_dim(x, (me ^ k) * piece, piece, dim), axis, k)
        for k in range(1, n)
    ]
    for g in got:
        total = total + g
    return total


def gather_direct(x, axis, dim):
    n = lax.axis_size(axis)
    me = lax.axis_index(axis)
    got = [x] + [swap(x, axis, k) for k in range(1, n)]
    for k in bits(n):
        bit = (me // k) % 2 == 1
        got = [jnp.where(bit, got[j ^ k], got[j]) for j in range(n)]
    return jnp.concatenate(got, dim)


def all_sum(x):
    x = halve(x, "dom", 1, 0)
    x = scatter_direct(x, "band", 0)
    for k in bits(lax.axis_size("dom"))[1:]:
        x = x + swap(x, "dom", k)
    x = gather_direct(x, "band", 0)
    return double(x, "dom", 1, 0)


def shards(block, locked):
    width = block.shape[1]
    part = width // CHUNKS
    nband = lax.axis_size("band")
    total_rows = block.shape[0] * lax.axis_size("dom")
    own = block.T
    parts = split(locked)
    owns = [own[c * part : (c + 1) * part] for c in range(CHUNKS)]
    wholes = [gather_direct(o, "band", 0) for o in owns]
    first = [dom_sum(product(parts, w, 0)) for w in wholes]
    terms = [scatter_direct(product(parts, c, 1), "band", 0) for c in first]
    once = [gather_direct(o - t, "band", 0) for o, t in zip(owns, terms)]
    second = [dom_sum(product(parts, w, 0)) for w in once]
    terms = [scatter_direct(product(parts, c, 1), "band", 1) for c in second]
    rows = terms[0].shape[1]
    start = lax.axis_index("band") * rows
    twice = [lax.dynamic_slice_in_dim(o, start, rows, 1) - t for o, t in zip(once, terms)]

    def ordered(xs):
        return jnp.concatenate(
            [x[b * part : (b + 1) * part] for b in range(nband) for x in xs], 0
        )

    mine = ordered(twice)
    gram_part = lax.dot_general(
        mine,
        mine,
        (((1,), (1,)), ((), ())),
        precision=lax.Precision.HIGHEST,
        preferred_element_type=f32,
    )
    gram = all_sum(gram_part) / total_rows
    whole = gather_direct(mine, "band", 1)
    coefficients = ordered([a + b for a, b in zip(first, second)]).T
    lower = jnp.linalg.cholesky(gram)
    solved = jax.scipy.linalg.solve_triangular(lower, whole, lower=True)
    basis = lax.dynamic_slice_in_dim(solved, lax.axis_index("band") * width, width, 0).T
    return (basis, coefficients)


def solution(mesh):
    placed = (P("dom", "band"), P("dom", "band"))
    return jax.shard_map(
        shards,
        mesh=mesh,
        in_specs=placed,
        out_specs=(P("dom", "band"), P("band", None)),
        check_vma=False,
    )
```

```python
import functools

import jax
import jax.numpy as jnp
from jax import lax
from jax.experimental import pallas as pl
from jax.experimental.pallas import tpu as pltpu
from jax.sharding import PartitionSpec as P

CHUNKS = 2
f32 = jnp.float32


def swap(x, axis, k):
    n = lax.axis_size(axis)
    return lax.ppermute(x, axis, [(i, i ^ k) for i in range(n)])


def bits(n):
    return [1 << i for i in range(n.bit_length() - 1)]


def split(x):
    hi = lax.reduce_precision(x, 8, 7)
    return hi.astype(jnp.bfloat16), (x - hi).astype(jnp.bfloat16)


def product(parts, w, dim):
    high, low = parts
    w_high, w_low = split(w)
    n = w.shape[0]
    dims = (((1,), (dim,)), ((), ()))
    both = lax.dot_general(
        jnp.concatenate([w_high, w_low], 0), high, dims, preferred_element_type=f32
    )
    rest = lax.dot_general(w_high, low, dims, preferred_element_type=f32)
    return both[:n] + (both[n:] + rest)


def halve(x, axis, k, dim):
    half = x.shape[dim] // 2
    bit = (lax.axis_index(axis) // k) % 2
    send = lax.dynamic_slice_in_dim(x, (1 - bit) * half, half, dim)
    keep = lax.dynamic_slice_in_dim(x, bit * half, half, dim)
    return keep + swap(send, axis, k)


def double(x, axis, k, dim):
    bit = (lax.axis_index(axis) // k) % 2 == 1
    other = swap(x, axis, k)
    return jnp.concatenate([jnp.where(bit, other, x), jnp.where(bit, x, other)], dim)


def dom_sum(x):
    ks = bits(lax.axis_size("dom"))
    for k in ks:
        x = halve(x, "dom", k, 0)
    for k in reversed(ks):
        x = double(x, "dom", k, 0)
    return x


def scatter_direct(x, axis, dim):
    n = lax.axis_size(axis)
    me = lax.axis_index(axis)
    piece = x.shape[dim] // n
    total = lax.dynamic_slice_in_dim(x, me * piece, piece, dim)
    got = [
        swap(lax.dynamic_slice_in_dim(x, (me ^ k) * piece, piece, dim), axis, k)
        for k in range(1, n)
    ]
    for g in got:
        total = total + g
    return total


def gather_direct(x, axis, dim):
    n = lax.axis_size(axis)
    me = lax.axis_index(axis)
    got = [x] + [swap(x, axis, k) for k in range(1, n)]
    for k in bits(n):
        bit = (me // k) % 2 == 1
        got = [jnp.where(bit, got[j ^ k], got[j]) for j in range(n)]
    return jnp.concatenate(got, dim)


def all_sum(x):
    x = halve(x, "dom", 1, 0)
    x = scatter_direct(x, "band", 0)
    for k in bits(lax.axis_size("dom"))[1:]:
        x = x + swap(x, "dom", k)
    x = gather_direct(x, "band", 0)
    return double(x, "dom", 1, 0)


def mm(a, b, ca, cb):
    dims = (((ca,), (cb,)), ((), ()))
    return lax.dot_general(
        a, b, dims, precision=lax.Precision.HIGHEST, preferred_element_type=f32
    )


def small_factor(square, group):
    s = square.shape[0]
    n = 2 * s
    eye = lax.broadcasted_iota(jnp.int32, (s, s), 0) == lax.broadcasted_iota(jnp.int32, (s, s), 1)
    full = jnp.concatenate([square, jnp.where(eye, 1.0, 0.0).astype(f32)], 1)
    rid = lax.broadcasted_iota(jnp.int32, (s, n), 0)
    lid = lax.broadcasted_iota(jnp.int32, (s, n), 1)

    def tall(x):
        return jnp.concatenate([x] * (s // 8), 0)

    for j in range(0, s, group):
        cols = [jnp.broadcast_to(full[:, j + a : j + a + 1], (s, n)) for a in range(group)]
        rows = [jnp.broadcast_to(full[j + a : j + a + 1, :], (8, n)) for a in range(group)]
        pivots = [
            [jnp.broadcast_to(cols[b][j + a : j + a + 1, :], (8, n)) for b in range(group)]
            for a in range(group)
        ]
        for a in range(group):
            inv = 1.0 / pivots[a][a]
            for r in range(a + 1, group):
                m = pivots[r][a] * inv
                for c in range(a + 1, group):
                    pivots[r][c] = pivots[r][c] - m * pivots[a][c]
                rows[r] = rows[r] - m * rows[a]
            factor = jnp.where(rid > j + a, cols[a] * tall(inv), 0.0)
            for c in range(a + 1, group):
                cols[c] = cols[c] - factor * tall(pivots[a][c])
            full = full - factor * tall(rows[a])
    diag = jnp.sum(jnp.where(rid == lid, full, 0.0), axis=1, keepdims=True)
    root = lax.rsqrt(diag)
    root = root * (1.5 - 0.5 * diag * root * root)
    return full[:, s:] * root


def factor_kernel(gram_ref, out_ref, rest_ref, *, scale, size, group):
    n = gram_ref.shape[0]
    rest_ref[...] = gram_ref[...] * scale
    eye = lax.broadcasted_iota(jnp.int32, (n, n), 0) == lax.broadcasted_iota(jnp.int32, (n, n), 1)
    out_ref[...] = jnp.where(eye, 1.0, 0.0).astype(f32)
    for p in range(0, n, size):
        e = p + size
        x = small_factor(rest_ref[p:e, p:e], group)
        y = mm(x, out_ref[p:e, :], 1, 0)
        if e < n:
            w = mm(x, rest_ref[p:e, :], 1, 0)
            below = w[:, e:]
            rest_ref[e:, :] = rest_ref[e:, :] - mm(below, w, 0, 0)
            out_ref[e:, :] = out_ref[e:, :] - mm(below, y, 0, 0)
        out_ref[p:e, :] = y


def inverse_factor(gram, scale):
    n = gram.shape[0]
    return pl.pallas_call(
        functools.partial(factor_kernel, scale=scale, size=64, group=8),
        out_shape=jax.ShapeDtypeStruct((n, n), f32),
        in_specs=[pl.BlockSpec(memory_space=pltpu.VMEM)],
        out_specs=pl.BlockSpec(memory_space=pltpu.VMEM),
        scratch_shapes=[pltpu.VMEM((n, n), f32)],
        compiler_params=pltpu.CompilerParams(vmem_limit_bytes=16 << 20),
        name="inverse_factor",
    )(gram)


def shards(block, locked):
    width = block.shape[1]
    part = width // CHUNKS
    nband = lax.axis_size("band")
    total_rows = block.shape[0] * lax.axis_size("dom")
    own = block.T
    parts = split(locked)
    owns = [own[c * part : (c + 1) * part] for c in range(CHUNKS)]
    wholes = [gather_direct(o, "band", 0) for o in owns]
    first = [dom_sum(product(parts, w, 0)) for w in wholes]
    terms = [scatter_direct(product(parts, c, 1), "band", 0) for c in first]
    once = [gather_direct(o - t, "band", 0) for o, t in zip(owns, terms)]
    second = [dom_sum(product(parts, w, 0)) for w in once]
    terms = [scatter_direct(product(parts, c, 1), "band", 1) for c in second]
    rows = terms[0].shape[1]
    start = lax.axis_index("band") * rows
    twice = [lax.dynamic_slice_in_dim(o, start, rows, 1) - t for o, t in zip(once, terms)]

    def ordered(xs):
        return jnp.concatenate(
            [x[b * part : (b + 1) * part] for b in range(nband) for x in xs], 0
        )

    mine = ordered(twice)
    gram = all_sum(mm(mine, mine, 1, 1))
    whole = gather_direct(mine, "band", 1)
    coefficients = ordered([a + b for a, b in zip(first, second)]).T
    inverse = inverse_factor(gram, 1.0 / total_rows)
    own_rows = lax.dynamic_slice_in_dim(inverse, lax.axis_index("band") * width, width, 0)
    basis = mm(own_rows, whole, 1, 0).T
    return (basis, coefficients)


def solution(mesh):
    placed = (P("dom", "band"), P("dom", "band"))
    return jax.shard_map(
        shards,
        mesh=mesh,
        in_specs=placed,
        out_specs=(P("dom", "band"), P("band", None)),
        check_vma=False,
    )
```

```python
import functools

import jax
import jax.numpy as jnp
from jax import lax
from jax.experimental import pallas as pl
from jax.experimental.pallas import tpu as pltpu
from jax.sharding import PartitionSpec as P

CHUNKS = 2
TURNS = "AAABABABABABABABABABABBB"
f32 = jnp.float32


def swap(x, axis, k):
    n = lax.axis_size(axis)
    return lax.ppermute(x, axis, [(i, i ^ k) for i in range(n)])


def bits(n):
    return [1 << i for i in range(n.bit_length() - 1)]


VMEM = pl.BlockSpec(memory_space=pltpu.VMEM)
SMEM = pl.BlockSpec(memory_space=pltpu.SMEM)
HBM = pl.BlockSpec(memory_space=pl.ANY)
LIMIT = pltpu.CompilerParams(vmem_limit_bytes=8 << 20)
SLOTS = 4


def split(x):
    high = x.astype(jnp.bfloat16)
    return high, (x - high.astype(f32)).astype(jnp.bfloat16)


def split_kernel(x_ref, parts_ref, slots, sems):
    size = slots.shape[1]
    count = x_ref.shape[0] // size

    def copy(i):
        return pltpu.make_async_copy(
            x_ref.at[pl.ds(i * size, size)], slots.at[i % SLOTS], sems.at[i % SLOTS]
        )

    for i in range(min(SLOTS, count)):
        copy(i).start()
    for i in range(count):
        copy(i).wait()
        high, low = split(slots[i % SLOTS])
        parts_ref[0, pl.ds(i * size, size), :] = high
        parts_ref[1, pl.ds(i * size, size), :] = low
        if i + SLOTS < count:
            copy(i + SLOTS).start()


def split_array(x):
    size = 128
    return pl.pallas_call(
        split_kernel,
        out_shape=jax.ShapeDtypeStruct((2, *x.shape), jnp.bfloat16),
        in_specs=[HBM],
        out_specs=VMEM,
        scratch_shapes=[
            pltpu.VMEM((SLOTS, size, x.shape[1]), f32),
            pltpu.SemaphoreType.DMA((SLOTS,)),
        ],
        compiler_params=LIMIT,
        name="split_array",
    )(x)


def product_kernel(place_ref, *refs, spans, dim, block, by_rows):
    count = len(spans)
    ins, parts, outs = refs[:count], refs[count], refs[count + 1 : -2]
    rows_ref, both_ref = refs[-2:]
    mask = place_ref[0]
    n = rows_ref.shape[0]
    w = 0
    for ref, span in zip(ins, spans):
        for i in range(*span, block):
            at = pl.multiple_of((w ^ mask) * block, block)
            rows_ref[pl.ds(at, block), :] = ref[i : i + block, :]
            w += 1
    both_ref[:n, :], both_ref[n:, :] = split(rows_ref[...])
    dims = (((1,), (dim,)), ((), ()))

    def slab(ref, start, size):
        if dim == 0:
            return parts[ref, :, pl.ds(start, size)]
        return parts[ref, pl.ds(start, size), :]

    def multiply(start, size):
        part = lax.dot_general(
            both_ref[...], slab(0, start, size), dims, preferred_element_type=f32
        )
        rest = lax.dot_general(
            both_ref[:n, :], slab(1, start, size), dims, preferred_element_type=f32
        )
        return part[:n] + (part[n:] + rest)

    width = parts.shape[2 - dim]
    if by_rows:
        size = width // len(outs)
        for k, out in enumerate(outs):
            at = pl.multiple_of((place_ref[1] ^ k) * size, size)
            out[...] = multiply(at, size)
    else:
        size = min(512, width)
        piece = n // len(outs)
        for start in range(0, width, size):
            got = multiply(start, size)
            for k, out in enumerate(outs):
                out[:, start : start + size] = got[k * piece : (k + 1) * piece]


def product(place, ins, parts, dim, block, pieces, by_rows=False, span=None):
    spans = [span or (0, x.shape[0]) for x in ins]
    n = sum(end - start for start, end in spans)
    depth = ins[0].shape[1]
    width = parts.shape[2 - dim]
    shape = (n, width // pieces) if by_rows else (n // pieces, width)
    return pl.pallas_call(
        functools.partial(
            product_kernel, spans=spans, dim=dim, block=block, by_rows=by_rows
        ),
        out_shape=[jax.ShapeDtypeStruct(shape, f32)] * pieces,
        in_specs=[SMEM] + [VMEM] * (len(ins) + 1),
        out_specs=[VMEM] * pieces,
        scratch_shapes=[pltpu.VMEM((n, depth), f32), pltpu.VMEM((2 * n, depth), jnp.bfloat16)],
        compiler_params=LIMIT,
        name="product_rows" if by_rows else f"product_{dim}",
    )(place, *ins, parts)


def coefficients_kernel(place_ref, *refs, block, width, count):
    *ins, out_ref, all_ref = refs
    mask = place_ref[0]
    nparts = len(ins) // (2 * count)
    for c in range(count):
        firsts = ins[2 * c * nparts : (2 * c + 1) * nparts]
        seconds = ins[(2 * c + 1) * nparts : (2 * c + 2) * nparts]
        v = 0
        for f, s in zip(firsts, seconds):
            for i in range(0, f.shape[0], block):
                u = (v ^ mask) * block
                part = width // count
                at = (u // part) * width + c * part + u % part
                at = pl.multiple_of(at, block)
                all_ref[pl.ds(at, block), :] = f[i : i + block, :] + s[i : i + block, :]
                v += 1
    size = min(512, out_ref.shape[0])
    for start in range(0, out_ref.shape[0], size):
        out_ref[start : start + size, :] = all_ref[:, start : start + size].T


def coefficients_of(place, pairs, block, width):
    ins = [x for first, second in pairs for x in (*first, *second)]
    n = sum(x.shape[0] for x in ins) // 2
    depth = ins[0].shape[1]
    return pl.pallas_call(
        functools.partial(coefficients_kernel, block=block, width=width, count=len(pairs)),
        out_shape=jax.ShapeDtypeStruct((depth, n), f32),
        in_specs=[SMEM] + [VMEM] * len(ins),
        out_specs=VMEM,
        scratch_shapes=[pltpu.VMEM((n, depth), f32)],
        compiler_params=LIMIT,
        name="coefficients",
    )(place, *ins)


def send_half(x, axis, k, dim):
    half = x.shape[dim] // 2
    bit = (lax.axis_index(axis) // k) % 2
    return swap(lax.dynamic_slice_in_dim(x, (1 - bit) * half, half, dim), axis, k)


def keep_half(x, got, axis, k, dim):
    half = x.shape[dim] // 2
    bit = (lax.axis_index(axis) // k) % 2
    return lax.dynamic_slice_in_dim(x, bit * half, half, dim) + got


def join(x, got, axis, k, dim):
    bit = (lax.axis_index(axis) // k) % 2 == 1
    return jnp.concatenate([jnp.where(bit, got, x), jnp.where(bit, x, got)], dim)


def send_pieces(x, axis, dim):
    n = lax.axis_size(axis)
    me = lax.axis_index(axis)
    piece = x.shape[dim] // n
    return [
        swap(lax.dynamic_slice_in_dim(x, (me ^ k) * piece, piece, dim), axis, k)
        for k in range(1, n)
    ]


def keep_piece(x, got, axis, dim):
    piece = x.shape[dim] // lax.axis_size(axis)
    total = lax.dynamic_slice_in_dim(x, lax.axis_index(axis) * piece, piece, dim)
    for g in got:
        total = total + g
    return total


def send_all(x, axis):
    return [swap(x, axis, k) for k in range(1, lax.axis_size(axis))]


def join_all(x, got, axis, dim):
    n = lax.axis_size(axis)
    me = lax.axis_index(axis)
    got = [x] + got
    for k in bits(n):
        bit = (me // k) % 2 == 1
        got = [jnp.where(bit, got[j ^ k], got[j]) for j in range(n)]
    return jnp.concatenate(got, dim)


def all_sum(x):
    x = keep_half(x, send_half(x, "dom", 1, 0), "dom", 1, 0)
    x = keep_piece(x, send_pieces(x, "band", 0), "band", 0)
    total = x
    for k in range(1, lax.axis_size("dom") // 2):
        total = total + swap(x, "dom", 2 * k)
    x = join_all(total, send_all(total, "band"), "band", 0)
    return join(x, swap(x, "dom", 1), "dom", 1, 0)


class Order:
    def __init__(self):
        self.last = ()

    def after(self, *xs):
        got = lax.optimization_barrier((xs, self.last))[0]
        return got if len(got) > 1 else got[0]

    def done(self, *xs):
        self.last = xs


def sweep(order, whole, span, parts, masks, last):
    nband, ndom = lax.axis_size("band"), lax.axis_size("dom")
    to_dom, to_band, to_columns = masks
    n = (span[1] - span[0]) * nband
    block = n // ndom
    keep, send = product(to_dom, whole, parts, 0, block, 2, span=span)
    got = swap(send, "dom", 1)
    order.done(keep)
    yield None
    keep, got = order.after(keep, got)
    mine = [keep[i : i + block] + got[i : i + block] for i in range(0, n // 2, block)]
    got = [swap(mine[k], "dom", 2 * k) for k in range(1, ndom // 2)]
    order.done(*mine)
    yield None
    mine, *got = order.after(mine[0], *got)
    for g in got:
        mine = mine + g
    got = [swap(mine, "dom", 2 * k) for k in range(1, ndom // 2)]
    order.done(mine)
    yield None
    half = jnp.concatenate(order.after(mine, *got), 0)
    got = swap(half, "dom", 1)
    order.done(half)
    yield None
    coef = order.after(half, got)
    if last:
        terms = product(to_columns, coef, parts, 1, block, nband, by_rows=True)
    else:
        terms = product(to_band, coef, parts, 1, block, nband)
    got = [swap(terms[k], "band", k) for k in range(1, nband)]
    order.done(*terms)
    yield None
    total, *got = order.after(terms[0], *got)
    for g in got:
        total = total + g
    yield coef, total


def chunk(order, whole, span, parts, masks):
    whole = order.after(*whole)
    for out in sweep(order, whole, span, parts, masks, False):
        if out is None:
            yield None
    first, terms = out
    own = whole[0][span[0] : span[1]] - terms
    got = send_all(own, "band")
    order.done(own)
    yield None
    once = order.after(own, *got)
    for out in sweep(order, once, (0, own.shape[0]), parts, masks, True):
        if out is None:
            yield None
    second, terms = out
    rows = terms.shape[1]
    start = lax.axis_index("band") * rows
    mine = [lax.dynamic_slice_in_dim(o, start, rows, 1) for o in once]
    yield (first, second), join_all(mine[0], mine[1:], "band", 0) - terms


def mm(a, b, ca, cb):
    dims = (((ca,), (cb,)), ((), ()))
    return lax.dot_general(
        a, b, dims, precision=lax.Precision.HIGHEST, preferred_element_type=f32
    )


def small_factor(square, group):
    s = square.shape[0]
    n = 2 * s
    eye = lax.broadcasted_iota(jnp.int32, (s, s), 0) == lax.broadcasted_iota(jnp.int32, (s, s), 1)
    full = jnp.concatenate([square, jnp.where(eye, 1.0, 0.0).astype(f32)], 1)
    rid = lax.broadcasted_iota(jnp.int32, (s, n), 0)
    lid = lax.broadcasted_iota(jnp.int32, (s, n), 1)

    def tall(x):
        return jnp.concatenate([x] * (s // 8), 0)

    for j in range(0, s, group):
        cols = [jnp.broadcast_to(full[:, j + a : j + a + 1], (s, n)) for a in range(group)]
        rows = [jnp.broadcast_to(full[j + a : j + a + 1, :], (8, n)) for a in range(group)]
        pivots = [
            [jnp.broadcast_to(cols[b][j + a : j + a + 1, :], (8, n)) for b in range(group)]
            for a in range(group)
        ]
        for a in range(group):
            inv = 1.0 / pivots[a][a]
            for r in range(a + 1, group):
                m = pivots[r][a] * inv
                for c in range(a + 1, group):
                    pivots[r][c] = pivots[r][c] - m * pivots[a][c]
                rows[r] = rows[r] - m * rows[a]
            factor = jnp.where(rid > j + a, cols[a] * tall(inv), 0.0)
            for c in range(a + 1, group):
                cols[c] = cols[c] - factor * tall(pivots[a][c])
            full = full - factor * tall(rows[a])
    diag = jnp.sum(jnp.where(rid == lid, full, 0.0), axis=1, keepdims=True)
    root = lax.rsqrt(diag)
    root = root * (1.5 - 0.5 * diag * root * root)
    return full[:, s:] * root


def factor_kernel(gram_ref, out_ref, rest_ref, *, scale, size, group):
    n = gram_ref.shape[0]
    rest_ref[...] = gram_ref[...] * scale
    eye = lax.broadcasted_iota(jnp.int32, (n, n), 0) == lax.broadcasted_iota(jnp.int32, (n, n), 1)
    out_ref[...] = jnp.where(eye, 1.0, 0.0).astype(f32)
    for p in range(0, n, size):
        e = p + size
        x = small_factor(rest_ref[p:e, p:e], group)
        y = mm(x, out_ref[p:e, :], 1, 0)
        if e < n:
            w = mm(x, rest_ref[p:e, :], 1, 0)
            below = w[:, e:]
            rest_ref[e:, :] = rest_ref[e:, :] - mm(below, w, 0, 0)
            out_ref[e:, :] = out_ref[e:, :] - mm(below, y, 0, 0)
        out_ref[p:e, :] = y


def inverse_factor(gram, scale):
    n = gram.shape[0]
    return pl.pallas_call(
        functools.partial(factor_kernel, scale=scale, size=64, group=8),
        out_shape=jax.ShapeDtypeStruct((n, n), f32),
        in_specs=[pl.BlockSpec(memory_space=pltpu.VMEM)],
        out_specs=pl.BlockSpec(memory_space=pltpu.VMEM),
        scratch_shapes=[pltpu.VMEM((n, n), f32)],
        compiler_params=pltpu.CompilerParams(vmem_limit_bytes=16 << 20),
        name="inverse_factor",
    )(gram)


def shards(block, locked):
    width = block.shape[1]
    part = width // CHUNKS
    nband = lax.axis_size("band")
    total_rows = block.shape[0] * lax.axis_size("dom")
    own = block.T
    dom, band, ndom = lax.axis_index("dom"), lax.axis_index("band"), lax.axis_size("dom")
    by_dom = (dom % 2) * (ndom // 2) + dom // 2
    by_band = band * (ndom // nband)
    masks = [
        jnp.stack([m, band]).astype(jnp.int32)
        for m in (by_dom ^ by_band, by_dom ^ by_band, by_dom)
    ]
    parts = split_array(locked)
    order = Order()
    blocks = [own] + send_all(own, "band")
    spans = [(c * part, (c + 1) * part) for c in range(CHUNKS)]
    runs = [chunk(order, blocks, span, parts, masks) for span in spans]
    out = [None] * CHUNKS
    for c in TURNS:
        out["AB".index(c)] = next(runs["AB".index(c)])
    sums, twice = zip(*out)

    def ordered(xs):
        return jnp.concatenate(
            [x[b * part : (b + 1) * part] for b in range(nband) for x in xs], 0
        )

    mine = ordered(twice)
    block_rows = part * nband // ndom

    gram = all_sum(mm(mine, mine, 1, 1))
    coefficients = coefficients_of(masks[2], sums, block_rows, width)
    whole = join_all(mine, send_all(mine, "band"), "band", 1)
    inverse = inverse_factor(gram, 1.0 / total_rows)
    own_rows = lax.dynamic_slice_in_dim(inverse, lax.axis_index("band") * width, width, 0)
    basis = mm(own_rows, whole, 1, 0).T
    return (basis, coefficients)


def solution(mesh):
    placed = (P("dom", "band"), P("dom", "band"))
    return jax.shard_map(
        shards,
        mesh=mesh,
        in_specs=placed,
        out_specs=(P("dom", "band"), P("band", None)),
        check_vma=False,
    )
```

```python
import functools

import jax
import jax.numpy as jnp
from jax import lax
from jax.experimental import pallas as pl
from jax.experimental.pallas import tpu as pltpu
from jax.sharding import PartitionSpec as P

CHUNKS = 2
TURNS = "AAABABABABABABABABABBBAB"
f32 = jnp.float32


def swap(x, axis, k):
    n = lax.axis_size(axis)
    return lax.ppermute(x, axis, [(i, i ^ k) for i in range(n)])


def bits(n):
    return [1 << i for i in range(n.bit_length() - 1)]


VMEM = pl.BlockSpec(memory_space=pltpu.VMEM)
SMEM = pl.BlockSpec(memory_space=pltpu.SMEM)
HBM = pl.BlockSpec(memory_space=pltpu.HBM)
LIMIT = pltpu.CompilerParams(vmem_limit_bytes=10 << 20)
SLOTS = 4


def split(x):
    high = x.astype(jnp.bfloat16)
    return high, (x - high.astype(f32)).astype(jnp.bfloat16)


def split_kernel(x_ref, parts_ref, slots, halves, sems, outs):
    size = slots.shape[1]
    count = x_ref.shape[0] // size

    def copy(i):
        return pltpu.make_async_copy(
            x_ref.at[pl.ds(i * size, size)], slots.at[i % SLOTS], sems.at[i % SLOTS]
        )

    def back(i, which):
        return pltpu.make_async_copy(
            halves.at[i % SLOTS, which],
            parts_ref.at[which, pl.ds(i * size, size)],
            outs.at[i % SLOTS, which],
        )

    for i in range(min(SLOTS, count)):
        copy(i).start()
    for i in range(count):
        copy(i).wait()
        if i >= SLOTS:
            back(i - SLOTS, 0).wait()
            back(i - SLOTS, 1).wait()
        halves[i % SLOTS, 0], halves[i % SLOTS, 1] = split(slots[i % SLOTS])
        back(i, 0).start()
        back(i, 1).start()
        if i + SLOTS < count:
            copy(i + SLOTS).start()
    for i in range(max(count - SLOTS, 0), count):
        back(i, 0).wait()
        back(i, 1).wait()


def split_array(x):
    size = 128
    return pl.pallas_call(
        split_kernel,
        out_shape=pltpu.HBM((2, *x.shape), jnp.bfloat16),
        in_specs=[HBM],
        out_specs=HBM,
        scratch_shapes=[
            pltpu.VMEM((SLOTS, size, x.shape[1]), f32),
            pltpu.VMEM((SLOTS, 2, size, x.shape[1]), jnp.bfloat16),
            pltpu.SemaphoreType.DMA((SLOTS,)),
            pltpu.SemaphoreType.DMA((SLOTS, 2)),
        ],
        compiler_params=LIMIT,
        name="split_array",
    )(x)


def product_kernel(place_ref, *refs, spans, dim, block, by_rows):
    count = len(spans)
    ins, parts, outs = refs[:count], refs[count], refs[count + 1 : -2]
    rows_ref, both_ref = refs[-2:]
    mask = place_ref[0]
    n = rows_ref.shape[0]
    w = 0
    for ref, span in zip(ins, spans):
        for i in range(*span, block):
            at = pl.multiple_of((w ^ mask) * block, block)
            rows_ref[pl.ds(at, block), :] = ref[i : i + block, :]
            w += 1
    both_ref[:n, :], both_ref[n:, :] = split(rows_ref[...])
    dims = (((1,), (dim,)), ((), ()))

    def slab(ref, start, size):
        if dim == 0:
            return parts[ref, :, pl.ds(start, size)]
        return parts[ref, pl.ds(start, size), :]

    def multiply(start, size):
        part = lax.dot_general(
            both_ref[...], slab(0, start, size), dims, preferred_element_type=f32
        )
        rest = lax.dot_general(
            both_ref[:n, :], slab(1, start, size), dims, preferred_element_type=f32
        )
        return part[:n] + (part[n:] + rest)

    width = parts.shape[2 - dim]
    if by_rows:
        size = width // len(outs)
        for k, out in enumerate(outs):
            at = pl.multiple_of((place_ref[1] ^ k) * size, size)
            out[...] = multiply(at, size)
    else:
        size = min(512, width)
        piece = n // len(outs)
        for start in range(0, width, size):
            got = multiply(start, size)
            for k, out in enumerate(outs):
                out[:, start : start + size] = got[k * piece : (k + 1) * piece]


def product(place, ins, parts, dim, block, pieces, by_rows=False, span=None):
    spans = [span or (0, x.shape[0]) for x in ins]
    n = sum(end - start for start, end in spans)
    depth = ins[0].shape[1]
    width = parts.shape[2 - dim]
    shape = (n, width // pieces) if by_rows else (n // pieces, width)
    return pl.pallas_call(
        functools.partial(
            product_kernel, spans=spans, dim=dim, block=block, by_rows=by_rows
        ),
        out_shape=[jax.ShapeDtypeStruct(shape, f32)] * pieces,
        in_specs=[SMEM] + [VMEM] * (len(ins) + 1),
        out_specs=[VMEM] * pieces,
        scratch_shapes=[pltpu.VMEM((n, depth), f32), pltpu.VMEM((2 * n, depth), jnp.bfloat16)],
        compiler_params=LIMIT,
        name="product_rows" if by_rows else f"product_{dim}",
    )(place, *ins, parts)


def touch_kernel(parts_ref, out_ref):
    rows, columns = out_ref.shape
    out_ref[...] = parts_ref[0, :rows, :columns].astype(f32)


def touch(parts):
    return pl.pallas_call(
        touch_kernel,
        out_shape=jax.ShapeDtypeStruct((16, 128), f32),
        in_specs=[VMEM],
        out_specs=VMEM,
        compiler_params=LIMIT,
        name="touch",
    )(parts)


def coefficients_kernel(place_ref, *refs, block, width, count):
    *ins, out_ref, all_ref = refs
    mask = place_ref[0]
    nparts = len(ins) // (2 * count)
    for c in range(count):
        firsts = ins[2 * c * nparts : (2 * c + 1) * nparts]
        seconds = ins[(2 * c + 1) * nparts : (2 * c + 2) * nparts]
        v = 0
        for f, s in zip(firsts, seconds):
            for i in range(0, f.shape[0], block):
                u = (v ^ mask) * block
                part = width // count
                at = (u // part) * width + c * part + u % part
                at = pl.multiple_of(at, block)
                all_ref[pl.ds(at, block), :] = f[i : i + block, :] + s[i : i + block, :]
                v += 1
    size = min(512, out_ref.shape[0])
    for start in range(0, out_ref.shape[0], size):
        out_ref[start : start + size, :] = all_ref[:, start : start + size].T


def coefficients_of(place, pairs, block, width):
    ins = [x for first, second in pairs for x in (*first, *second)]
    n = sum(x.shape[0] for x in ins) // 2
    depth = ins[0].shape[1]
    return pl.pallas_call(
        functools.partial(coefficients_kernel, block=block, width=width, count=len(pairs)),
        out_shape=jax.ShapeDtypeStruct((depth, n), f32),
        in_specs=[SMEM] + [pl.BlockSpec(x.shape, lambda: (0, 0)) for x in ins],
        out_specs=pl.BlockSpec((depth, n), lambda: (0, 0)),
        scratch_shapes=[pltpu.VMEM((n, depth), f32)],
        compiler_params=pltpu.CompilerParams(vmem_limit_bytes=16 << 20),
        name="coefficients",
    )(place, *ins)


def send_half(x, axis, k, dim):
    half = x.shape[dim] // 2
    bit = (lax.axis_index(axis) // k) % 2
    return swap(lax.dynamic_slice_in_dim(x, (1 - bit) * half, half, dim), axis, k)


def keep_half(x, got, axis, k, dim):
    half = x.shape[dim] // 2
    bit = (lax.axis_index(axis) // k) % 2
    return lax.dynamic_slice_in_dim(x, bit * half, half, dim) + got


def join(x, got, axis, k, dim):
    bit = (lax.axis_index(axis) // k) % 2 == 1
    return jnp.concatenate([jnp.where(bit, got, x), jnp.where(bit, x, got)], dim)


def send_pieces(x, axis, dim):
    n = lax.axis_size(axis)
    me = lax.axis_index(axis)
    piece = x.shape[dim] // n
    return [
        swap(lax.dynamic_slice_in_dim(x, (me ^ k) * piece, piece, dim), axis, k)
        for k in range(1, n)
    ]


def keep_piece(x, got, axis, dim):
    piece = x.shape[dim] // lax.axis_size(axis)
    total = lax.dynamic_slice_in_dim(x, lax.axis_index(axis) * piece, piece, dim)
    for g in got:
        total = total + g
    return total


def send_all(x, axis):
    return [swap(x, axis, k) for k in range(1, lax.axis_size(axis))]


def join_all(x, got, axis, dim):
    n = lax.axis_size(axis)
    me = lax.axis_index(axis)
    got = [x] + got
    for k in bits(n):
        bit = (me // k) % 2 == 1
        got = [jnp.where(bit, got[j ^ k], got[j]) for j in range(n)]
    return jnp.concatenate(got, dim)


def all_sum(x):
    x = keep_half(x, send_half(x, "dom", 1, 0), "dom", 1, 0)
    x = keep_piece(x, send_pieces(x, "band", 0), "band", 0)
    total = x
    for k in range(1, lax.axis_size("dom") // 2):
        total = total + swap(x, "dom", 2 * k)
    x = join_all(total, send_all(total, "band"), "band", 0)
    return join(x, swap(x, "dom", 1), "dom", 1, 0)


class Order:
    def __init__(self):
        self.last = ()

    def after(self, *xs):
        got = lax.optimization_barrier((xs, self.last))[0]
        return got if len(got) > 1 else got[0]

    def done(self, *xs):
        self.last = xs


def sweep(order, whole, span, parts, masks, last):
    nband, ndom = lax.axis_size("band"), lax.axis_size("dom")
    to_dom, to_band, to_columns = masks
    n = (span[1] - span[0]) * nband
    block = n // ndom
    keep, send = product(to_dom, whole, parts, 0, block, 2, span=span)
    got = swap(send, "dom", 1)
    order.done(keep)
    yield None
    keep, got = order.after(keep, got)
    mine = [keep[i : i + block] + got[i : i + block] for i in range(0, n // 2, block)]
    got = [swap(mine[k], "dom", 2 * k) for k in range(1, ndom // 2)]
    order.done(*mine)
    yield None
    mine, *got = order.after(mine[0], *got)
    for g in got:
        mine = mine + g
    got = [swap(mine, "dom", 2 * k) for k in range(1, ndom // 2)]
    order.done(mine)
    yield None
    half = jnp.concatenate(order.after(mine, *got), 0)
    got = swap(half, "dom", 1)
    order.done(half)
    yield None
    coef = order.after(half, got)
    if last:
        terms = product(to_columns, coef, parts, 1, block, nband, by_rows=True)
    else:
        terms = product(to_band, coef, parts, 1, block, nband)
    got = [swap(terms[k], "band", k) for k in range(1, nband)]
    order.done(*terms)
    yield None
    total, *got = order.after(terms[0], *got)
    for g in got:
        total = total + g
    yield coef, total


def chunk(order, whole, span, parts, masks):
    whole = order.after(*whole)
    for out in sweep(order, whole, span, parts, masks, False):
        if out is None:
            yield None
    first, terms = out
    own = whole[0][span[0] : span[1]] - terms
    got = send_all(own, "band")
    order.done(own)
    yield None
    once = order.after(own, *got)
    for out in sweep(order, once, (0, own.shape[0]), parts, masks, True):
        if out is None:
            yield None
    second, terms = out
    rows = terms.shape[1]
    start = lax.axis_index("band") * rows
    mine = [lax.dynamic_slice_in_dim(o, start, rows, 1) for o in once]
    yield (first, second), join_all(mine[0], mine[1:], "band", 0) - terms


def mm(a, b, ca, cb):
    dims = (((ca,), (cb,)), ((), ()))
    return lax.dot_general(
        a, b, dims, precision=lax.Precision.HIGHEST, preferred_element_type=f32
    )


def small_factor(square, group):
    s = square.shape[0]
    n = 2 * s
    eye = lax.broadcasted_iota(jnp.int32, (s, s), 0) == lax.broadcasted_iota(jnp.int32, (s, s), 1)
    full = jnp.concatenate([square, jnp.where(eye, 1.0, 0.0).astype(f32)], 1)
    rid = lax.broadcasted_iota(jnp.int32, (s, n), 0)
    lid = lax.broadcasted_iota(jnp.int32, (s, n), 1)

    def tall(x):
        return jnp.concatenate([x] * (s // 8), 0)

    for j in range(0, s, group):
        cols = [jnp.broadcast_to(full[:, j + a : j + a + 1], (s, n)) for a in range(group)]
        rows = [jnp.broadcast_to(full[j + a : j + a + 1, :], (8, n)) for a in range(group)]
        pivots = [
            [jnp.broadcast_to(cols[b][j + a : j + a + 1, :], (8, n)) for b in range(group)]
            for a in range(group)
        ]
        for a in range(group):
            inv = 1.0 / pivots[a][a]
            for r in range(a + 1, group):
                m = pivots[r][a] * inv
                for c in range(a + 1, group):
                    pivots[r][c] = pivots[r][c] - m * pivots[a][c]
                rows[r] = rows[r] - m * rows[a]
            factor = jnp.where(rid > j + a, cols[a] * tall(inv), 0.0)
            for c in range(a + 1, group):
                cols[c] = cols[c] - factor * tall(pivots[a][c])
            full = full - factor * tall(rows[a])
    diag = jnp.sum(jnp.where(rid == lid, full, 0.0), axis=1, keepdims=True)
    root = lax.rsqrt(diag)
    root = root * (1.5 - 0.5 * diag * root * root)
    return full[:, s:] * root


def factor_kernel(gram_ref, out_ref, rest_ref, *, scale, size, group):
    n = gram_ref.shape[0]
    rest_ref[...] = gram_ref[...] * scale
    eye = lax.broadcasted_iota(jnp.int32, (n, n), 0) == lax.broadcasted_iota(jnp.int32, (n, n), 1)
    out_ref[...] = jnp.where(eye, 1.0, 0.0).astype(f32)
    for p in range(0, n, size):
        e = p + size
        x = small_factor(rest_ref[p:e, p:e], group)
        y = mm(x, out_ref[p:e, :], 1, 0)
        if e < n:
            w = mm(x, rest_ref[p:e, :], 1, 0)
            below = w[:, e:]
            rest_ref[e:, :] = rest_ref[e:, :] - mm(below, w, 0, 0)
            out_ref[e:, :] = out_ref[e:, :] - mm(below, y, 0, 0)
        out_ref[p:e, :] = y


def inverse_factor(gram, scale):
    n = gram.shape[0]
    return pl.pallas_call(
        functools.partial(factor_kernel, scale=scale, size=64, group=8),
        out_shape=jax.ShapeDtypeStruct((n, n), f32),
        in_specs=[pl.BlockSpec(memory_space=pltpu.VMEM)],
        out_specs=pl.BlockSpec(memory_space=pltpu.VMEM),
        scratch_shapes=[pltpu.VMEM((n, n), f32)],
        compiler_params=pltpu.CompilerParams(vmem_limit_bytes=16 << 20),
        name="inverse_factor",
    )(gram)


def shards(block, locked):
    width = block.shape[1]
    part = width // CHUNKS
    nband = lax.axis_size("band")
    total_rows = block.shape[0] * lax.axis_size("dom")
    own = block.T
    dom, band, ndom = lax.axis_index("dom"), lax.axis_index("band"), lax.axis_size("dom")
    by_dom = (dom % 2) * (ndom // 2) + dom // 2
    by_band = band * (ndom // nband)
    masks = [
        jnp.stack([m, band]).astype(jnp.int32)
        for m in (by_dom ^ by_band, by_dom ^ by_band, by_dom)
    ]
    parts = split_array(locked)
    order = Order()
    blocks = [own] + send_all(own, "band")
    spans = [(c * part, (c + 1) * part) for c in range(CHUNKS)]
    order.done(touch(parts))
    runs = [chunk(order, blocks, span, parts, masks) for span in spans]
    out = [None] * CHUNKS
    for c in TURNS:
        out["AB".index(c)] = next(runs["AB".index(c)])
    sums, twice = zip(*out)

    def ordered(xs):
        return jnp.concatenate(
            [x[b * part : (b + 1) * part] for b in range(nband) for x in xs], 0
        )

    mine = ordered(twice)
    block_rows = part * nband // ndom

    gram = all_sum(mm(mine, mine, 1, 1))
    whole = join_all(mine, send_all(mine, "band"), "band", 1)
    inverse = inverse_factor(gram, 1.0 / total_rows)
    flat = lax.optimization_barrier(([x for pair in sums for half in pair for x in half], inverse))[0]
    taken = iter(flat)
    pairs = [tuple(tuple(next(taken) for _ in half) for half in pair) for pair in sums]
    coefficients = coefficients_of(masks[2], pairs, block_rows, width)
    own_rows = lax.dynamic_slice_in_dim(inverse, lax.axis_index("band") * width, width, 0)
    basis = mm(own_rows, whole, 1, 0).T
    return (basis, coefficients)


def solution(mesh):
    placed = (P("dom", "band"), P("dom", "band"))
    return jax.shard_map(
        shards,
        mesh=mesh,
        in_specs=placed,
        out_specs=(P("dom", "band"), P("band", None)),
        check_vma=False,
    )
```

```python
import functools

import jax
import jax.numpy as jnp
from jax import lax
from jax.experimental import pallas as pl
from jax.experimental.pallas import tpu as pltpu
from jax.sharding import PartitionSpec as P

CHUNKS = 2
TURNS = "AAABABABABABABABABABBBAB"
f32 = jnp.float32


def swap(x, axis, k):
    n = lax.axis_size(axis)
    return lax.ppermute(x, axis, [(i, i ^ k) for i in range(n)])


def bits(n):
    return [1 << i for i in range(n.bit_length() - 1)]


VMEM = pl.BlockSpec(memory_space=pltpu.VMEM)
SMEM = pl.BlockSpec(memory_space=pltpu.SMEM)
HBM = pl.BlockSpec(memory_space=pltpu.HBM)
LIMIT = pltpu.CompilerParams(vmem_limit_bytes=10 << 20)
SLOTS = 4


def split(x):
    high = x.astype(jnp.bfloat16)
    return high, (x - high.astype(f32)).astype(jnp.bfloat16)


def split_kernel(x_ref, parts_ref, slots, halves, sems, outs):
    size = slots.shape[1]
    count = x_ref.shape[0] // size

    def copy(i):
        return pltpu.make_async_copy(
            x_ref.at[pl.ds(i * size, size)], slots.at[i % SLOTS], sems.at[i % SLOTS]
        )

    def back(i, which):
        return pltpu.make_async_copy(
            halves.at[i % SLOTS, which],
            parts_ref.at[which, pl.ds(i * size, size)],
            outs.at[i % SLOTS, which],
        )

    for i in range(min(SLOTS, count)):
        copy(i).start()
    for i in range(count):
        copy(i).wait()
        if i >= SLOTS:
            back(i - SLOTS, 0).wait()
            back(i - SLOTS, 1).wait()
        halves[i % SLOTS, 0], halves[i % SLOTS, 1] = split(slots[i % SLOTS])
        back(i, 0).start()
        back(i, 1).start()
        if i + SLOTS < count:
            copy(i + SLOTS).start()
    for i in range(max(count - SLOTS, 0), count):
        back(i, 0).wait()
        back(i, 1).wait()


def split_array(x):
    size = 128
    return pl.pallas_call(
        split_kernel,
        out_shape=pltpu.HBM((2, *x.shape), jnp.bfloat16),
        in_specs=[HBM],
        out_specs=HBM,
        scratch_shapes=[
            pltpu.VMEM((SLOTS, size, x.shape[1]), f32),
            pltpu.VMEM((SLOTS, 2, size, x.shape[1]), jnp.bfloat16),
            pltpu.SemaphoreType.DMA((SLOTS,)),
            pltpu.SemaphoreType.DMA((SLOTS, 2)),
        ],
        compiler_params=LIMIT,
        name="split_array",
    )(x)


def product_kernel(place_ref, *refs, spans, dim, block, by_rows):
    count = len(spans)
    ins, parts, outs = refs[:count], refs[count], refs[count + 1 : -2]
    rows_ref, both_ref = refs[-2:]
    mask = place_ref[0]
    n = rows_ref.shape[0]
    w = 0
    for ref, span in zip(ins, spans):
        for i in range(*span, block):
            at = pl.multiple_of((w ^ mask) * block, block)
            rows_ref[pl.ds(at, block), :] = ref[i : i + block, :]
            w += 1
    both_ref[:n, :], both_ref[n:, :] = split(rows_ref[...])
    dims = (((1,), (dim,)), ((), ()))

    def slab(ref, start, size):
        if dim == 0:
            return parts[ref, :, pl.ds(start, size)]
        return parts[ref, pl.ds(start, size), :]

    def multiply(start, size):
        part = lax.dot_general(
            both_ref[...], slab(0, start, size), dims, preferred_element_type=f32
        )
        rest = lax.dot_general(
            both_ref[:n, :], slab(1, start, size), dims, preferred_element_type=f32
        )
        return part[:n] + (part[n:] + rest)

    width = parts.shape[2 - dim]
    if by_rows:
        size = width // len(outs)
        for k, out in enumerate(outs):
            at = pl.multiple_of((place_ref[1] ^ k) * size, size)
            out[...] = multiply(at, size)
    else:
        size = min(1024, width)
        piece = n // len(outs)
        for start in range(0, width, size):
            got = multiply(start, size)
            for k, out in enumerate(outs):
                out[:, start : start + size] = got[k * piece : (k + 1) * piece]


def product(place, ins, parts, dim, block, pieces, by_rows=False, span=None):
    spans = [span or (0, x.shape[0]) for x in ins]
    n = sum(end - start for start, end in spans)
    depth = ins[0].shape[1]
    width = parts.shape[2 - dim]
    shape = (n, width // pieces) if by_rows else (n // pieces, width)
    return pl.pallas_call(
        functools.partial(
            product_kernel, spans=spans, dim=dim, block=block, by_rows=by_rows
        ),
        out_shape=[jax.ShapeDtypeStruct(shape, f32)] * pieces,
        in_specs=[SMEM] + [VMEM] * (len(ins) + 1),
        out_specs=[VMEM] * pieces,
        scratch_shapes=[pltpu.VMEM((n, depth), f32), pltpu.VMEM((2 * n, depth), jnp.bfloat16)],
        compiler_params=LIMIT,
        name="product_rows" if by_rows else f"product_{dim}",
    )(place, *ins, parts)


def touch_kernel(parts_ref, out_ref):
    rows, columns = out_ref.shape
    out_ref[...] = parts_ref[0, :rows, :columns].astype(f32)


def touch(parts):
    return pl.pallas_call(
        touch_kernel,
        out_shape=jax.ShapeDtypeStruct((16, 128), f32),
        in_specs=[VMEM],
        out_specs=VMEM,
        compiler_params=LIMIT,
        name="touch",
    )(parts)


def coefficients_kernel(place_ref, *refs, block, width, count):
    *ins, out_ref, all_ref = refs
    mask = place_ref[0]
    nparts = len(ins) // (2 * count)
    for c in range(count):
        firsts = ins[2 * c * nparts : (2 * c + 1) * nparts]
        seconds = ins[(2 * c + 1) * nparts : (2 * c + 2) * nparts]
        v = 0
        for f, s in zip(firsts, seconds):
            for i in range(0, f.shape[0], block):
                u = (v ^ mask) * block
                part = width // count
                at = (u // part) * width + c * part + u % part
                at = pl.multiple_of(at, block)
                all_ref[pl.ds(at, block), :] = f[i : i + block, :] + s[i : i + block, :]
                v += 1
    size = min(512, out_ref.shape[0])
    for start in range(0, out_ref.shape[0], size):
        out_ref[start : start + size, :] = all_ref[:, start : start + size].T


def coefficients_of(place, pairs, block, width):
    ins = [x for first, second in pairs for x in (*first, *second)]
    n = sum(x.shape[0] for x in ins) // 2
    depth = ins[0].shape[1]
    return pl.pallas_call(
        functools.partial(coefficients_kernel, block=block, width=width, count=len(pairs)),
        out_shape=jax.ShapeDtypeStruct((depth, n), f32),
        in_specs=[SMEM] + [pl.BlockSpec(x.shape, lambda: (0, 0)) for x in ins],
        out_specs=pl.BlockSpec((depth, n), lambda: (0, 0)),
        scratch_shapes=[pltpu.VMEM((n, depth), f32)],
        compiler_params=pltpu.CompilerParams(vmem_limit_bytes=16 << 20),
        name="coefficients",
    )(place, *ins)


def send_half(x, axis, k, dim):
    half = x.shape[dim] // 2
    bit = (lax.axis_index(axis) // k) % 2
    return swap(lax.dynamic_slice_in_dim(x, (1 - bit) * half, half, dim), axis, k)


def keep_half(x, got, axis, k, dim):
    half = x.shape[dim] // 2
    bit = (lax.axis_index(axis) // k) % 2
    return lax.dynamic_slice_in_dim(x, bit * half, half, dim) + got


def join(x, got, axis, k, dim):
    bit = (lax.axis_index(axis) // k) % 2 == 1
    return jnp.concatenate([jnp.where(bit, got, x), jnp.where(bit, x, got)], dim)


def send_pieces(x, axis, dim):
    n = lax.axis_size(axis)
    me = lax.axis_index(axis)
    piece = x.shape[dim] // n
    return [
        swap(lax.dynamic_slice_in_dim(x, (me ^ k) * piece, piece, dim), axis, k)
        for k in range(1, n)
    ]


def keep_piece(x, got, axis, dim):
    piece = x.shape[dim] // lax.axis_size(axis)
    total = lax.dynamic_slice_in_dim(x, lax.axis_index(axis) * piece, piece, dim)
    for g in got:
        total = total + g
    return total


def send_all(x, axis):
    return [swap(x, axis, k) for k in range(1, lax.axis_size(axis))]


def join_all(x, got, axis, dim):
    n = lax.axis_size(axis)
    me = lax.axis_index(axis)
    got = [x] + got
    for k in bits(n):
        bit = (me // k) % 2 == 1
        got = [jnp.where(bit, got[j ^ k], got[j]) for j in range(n)]
    return jnp.concatenate(got, dim)


def all_sum(x):
    x = keep_half(x, send_half(x, "dom", 1, 0), "dom", 1, 0)
    x = keep_piece(x, send_pieces(x, "band", 0), "band", 0)
    total = x
    for k in range(1, lax.axis_size("dom") // 2):
        total = total + swap(x, "dom", 2 * k)
    x = join_all(total, send_all(total, "band"), "band", 0)
    return join(x, swap(x, "dom", 1), "dom", 1, 0)


class Order:
    def __init__(self):
        self.last = ()

    def after(self, *xs):
        got = lax.optimization_barrier((xs, self.last))[0]
        return got if len(got) > 1 else got[0]

    def done(self, *xs):
        self.last = xs


def sweep(order, whole, span, parts, masks, last):
    nband, ndom = lax.axis_size("band"), lax.axis_size("dom")
    to_dom, to_band, to_columns = masks
    n = (span[1] - span[0]) * nband
    block = n // ndom
    keep, send = product(to_dom, whole, parts, 0, block, 2, span=span)
    got = swap(send, "dom", 1)
    order.done(keep)
    yield None
    keep, got = order.after(keep, got)
    mine = [keep[i : i + block] + got[i : i + block] for i in range(0, n // 2, block)]
    got = [swap(mine[k], "dom", 2 * k) for k in range(1, ndom // 2)]
    order.done(*mine)
    yield None
    mine, *got = order.after(mine[0], *got)
    for g in got:
        mine = mine + g
    got = [swap(mine, "dom", 2 * k) for k in range(1, ndom // 2)]
    order.done(mine)
    yield None
    half = jnp.concatenate(order.after(mine, *got), 0)
    got = swap(half, "dom", 1)
    order.done(half)
    yield None
    coef = order.after(half, got)
    if last:
        terms = product(to_columns, coef, parts, 1, block, nband, by_rows=True)
    else:
        terms = product(to_band, coef, parts, 1, block, nband)
    got = [swap(terms[k], "band", k) for k in range(1, nband)]
    order.done(*terms)
    yield None
    total, *got = order.after(terms[0], *got)
    for g in got:
        total = total + g
    yield coef, total


def chunk(order, whole, span, parts, masks):
    whole = order.after(*whole)
    for out in sweep(order, whole, span, parts, masks, False):
        if out is None:
            yield None
    first, terms = out
    own = whole[0][span[0] : span[1]] - terms
    got = send_all(own, "band")
    order.done(own)
    yield None
    once = order.after(own, *got)
    for out in sweep(order, once, (0, own.shape[0]), parts, masks, True):
        if out is None:
            yield None
    second, terms = out
    rows = terms.shape[1]
    start = lax.axis_index("band") * rows
    mine = [lax.dynamic_slice_in_dim(o, start, rows, 1) for o in once]
    yield (first, second), join_all(mine[0], mine[1:], "band", 0) - terms


def mm(a, b, ca, cb):
    dims = (((ca,), (cb,)), ((), ()))
    return lax.dot_general(
        a, b, dims, precision=lax.Precision.HIGHEST, preferred_element_type=f32
    )


def small_factor(square, group):
    s = square.shape[0]
    n = 2 * s
    eye = lax.broadcasted_iota(jnp.int32, (s, s), 0) == lax.broadcasted_iota(jnp.int32, (s, s), 1)
    full = jnp.concatenate([square, jnp.where(eye, 1.0, 0.0).astype(f32)], 1)
    rid = lax.broadcasted_iota(jnp.int32, (s, n), 0)
    lid = lax.broadcasted_iota(jnp.int32, (s, n), 1)

    def tall(x):
        return jnp.concatenate([x] * (s // 8), 0)

    for j in range(0, s, group):
        cols = [jnp.broadcast_to(full[:, j + a : j + a + 1], (s, n)) for a in range(group)]
        rows = [jnp.broadcast_to(full[j + a : j + a + 1, :], (8, n)) for a in range(group)]
        pivots = [
            [jnp.broadcast_to(cols[b][j + a : j + a + 1, :], (8, n)) for b in range(group)]
            for a in range(group)
        ]
        for a in range(group):
            inv = 1.0 / pivots[a][a]
            for r in range(a + 1, group):
                m = pivots[r][a] * inv
                for c in range(a + 1, group):
                    pivots[r][c] = pivots[r][c] - m * pivots[a][c]
                rows[r] = rows[r] - m * rows[a]
            factor = jnp.where(rid > j + a, cols[a] * tall(inv), 0.0)
            for c in range(a + 1, group):
                cols[c] = cols[c] - factor * tall(pivots[a][c])
            full = full - factor * tall(rows[a])
    diag = jnp.sum(jnp.where(rid == lid, full, 0.0), axis=1, keepdims=True)
    root = lax.rsqrt(diag)
    root = root * (1.5 - 0.5 * diag * root * root)
    return full[:, s:] * root


def factor_kernel(gram_ref, out_ref, rest_ref, *, scale, size, group):
    n = gram_ref.shape[0]
    rest_ref[...] = gram_ref[...] * scale
    eye = lax.broadcasted_iota(jnp.int32, (n, n), 0) == lax.broadcasted_iota(jnp.int32, (n, n), 1)
    out_ref[...] = jnp.where(eye, 1.0, 0.0).astype(f32)
    for p in range(0, n, size):
        e = p + size
        x = small_factor(rest_ref[p:e, p:e], group)
        y = mm(x, out_ref[p:e, :], 1, 0)
        if e < n:
            w = mm(x, rest_ref[p:e, :], 1, 0)
            below = w[:, e:]
            rest_ref[e:, :] = rest_ref[e:, :] - mm(below, w, 0, 0)
            out_ref[e:, :] = out_ref[e:, :] - mm(below, y, 0, 0)
        out_ref[p:e, :] = y


def inverse_factor(gram, scale):
    n = gram.shape[0]
    return pl.pallas_call(
        functools.partial(factor_kernel, scale=scale, size=64, group=8),
        out_shape=jax.ShapeDtypeStruct((n, n), f32),
        in_specs=[pl.BlockSpec(memory_space=pltpu.VMEM)],
        out_specs=pl.BlockSpec(memory_space=pltpu.VMEM),
        scratch_shapes=[pltpu.VMEM((n, n), f32)],
        compiler_params=pltpu.CompilerParams(vmem_limit_bytes=16 << 20),
        name="inverse_factor",
    )(gram)


def shards(block, locked):
    width = block.shape[1]
    part = width // CHUNKS
    nband = lax.axis_size("band")
    total_rows = block.shape[0] * lax.axis_size("dom")
    own = block.T
    dom, band, ndom = lax.axis_index("dom"), lax.axis_index("band"), lax.axis_size("dom")
    by_dom = (dom % 2) * (ndom // 2) + dom // 2
    by_band = band * (ndom // nband)
    masks = [
        jnp.stack([m, band]).astype(jnp.int32)
        for m in (by_dom ^ by_band, by_dom ^ by_band, by_dom)
    ]
    parts = split_array(locked)
    order = Order()
    blocks = [own] + send_all(own, "band")
    spans = [(c * part, (c + 1) * part) for c in range(CHUNKS)]
    order.done(touch(parts))
    runs = [chunk(order, blocks, span, parts, masks) for span in spans]
    out = [None] * CHUNKS
    for c in TURNS:
        out["AB".index(c)] = next(runs["AB".index(c)])
    sums, twice = zip(*out)

    def ordered(xs):
        return jnp.concatenate(
            [x[b * part : (b + 1) * part] for b in range(nband) for x in xs], 0
        )

    mine = ordered(twice)
    block_rows = part * nband // ndom

    gram = all_sum(mm(mine, mine, 1, 1))
    whole = join_all(mine, send_all(mine, "band"), "band", 1)
    inverse = inverse_factor(gram, 1.0 / total_rows)
    flat = lax.optimization_barrier(([x for pair in sums for half in pair for x in half], inverse))[0]
    taken = iter(flat)
    pairs = [tuple(tuple(next(taken) for _ in half) for half in pair) for pair in sums]
    coefficients = coefficients_of(masks[2], pairs, block_rows, width)
    own_rows = lax.dynamic_slice_in_dim(inverse, lax.axis_index("band") * width, width, 0)
    basis = mm(own_rows, whole, 1, 0).T
    return (basis, coefficients)


def solution(mesh):
    placed = (P("dom", "band"), P("dom", "band"))
    return jax.shard_map(
        shards,
        mesh=mesh,
        in_specs=placed,
        out_specs=(P("dom", "band"), P("band", None)),
        check_vma=False,
    )
```
